32 devices in a mesh: groups: 2 (over y), expert: 4 (over x, core), dp: 4 (over z).
Axes of the slice: x: 2, y: 2, z: 4, core: 2. Of those that a mesh axis runs over, the one named last changes fastest.
Arguments:
- hidden_in: bfloat16 [4096, 1024], P(('groups', 'expert', 'dp')), parts along dimension 0, may hold values from -125 to 125
- context: bfloat16 [4096, 1024], P(('groups', 'expert', 'dp')), parts along dimension 0, may hold values from -6 to 6
- norm_gain: float32 [1024], replicated, may hold values from 0.1 to 1.9
- route_ids: int32 [4096, 8], P(('groups', 'expert', 'dp')), parts along dimension 0, may hold values from 0 to 31, all different within a row; in each aligned block of 128 rows (0 to 127, 128 to 255, ...) at most 36 rows name the same one
- route_weights: float32 [4096, 8], P(('groups', 'expert', 'dp')), parts along dimension 0, may hold values from 0.03 to 0.4
- w_gate: bfloat16 [32, 1024, 512], P('expert'), may hold values from -0.1875 to 0.1875
- w_up: bfloat16 [32, 1024, 512], P('expert'), may hold values from -0.1875 to 0.1875
- w_down: bfloat16 [32, 512, 1024], P('expert'), may hold values from -0.25 to 0.25
- out_grad: bfloat16 [4096, 1024], P(('groups', 'expert', 'dp')), parts along dimension 0, may hold values from -6 to 6
Outputs:
- moe_out: bfloat16 [4096, 1024], P(('groups', 'expert', 'dp')), parts along dimension 0
- branch_grad: bfloat16 [4096, 1024], P(('groups', 'expert', 'dp')), parts along dimension 0
- route_grad: float32 [4096, 8], P(('groups', 'expert', 'dp')), parts along dimension 0
- gain_grad: float32 [2048], P(('groups', 'expert', 'dp')), parts along dimension 0
- proj_grad: float32 [2048, 1024], P(('groups', 'expert', 'dp')), parts along dimension 0
- gate_grad: float32 [64, 1024, 512], P(('groups', 'expert'), 'dp'), parts along dimension 0
- up_grad: float32 [64, 1024, 512], P(('groups', 'expert'), 'dp'), parts along dimension 0
- down_grad: float32 [64, 512, 1024], P(('groups', 'expert'), 'dp'), parts along dimension 0
The draws below stay inside these ranges and needn't reach their ends.
There are 2 independent parts, one for each index of `groups`. The reference program is written for one: setup_inputs(seed, part) draws one part's arguments, and reference() takes and returns one part's arrays. A program takes and returns all parts, laid end to end along the dimension named above; an argument that names none is the same for every part. Nothing has to cross between parts.
Inputs may be any that keep to these rules, and one draw needn't show every extreme that they name: `route_ids`: each row names 8 different experts; in each aligned block of 128 rows no expert is named by more than 36 rows, a bound that some block reaches.
All inputs are finite; a program needn't handle non-finite values.
Results may differ from the reference program's by a relative error of at most 0.0085.
Values may be sent and summed in bfloat16 or wider, within the bound.
A program may use at most 192 MiB of HBM per device.

```python
import math
import jax
import jax.numpy as jnp
import numpy as np
from jax import lax

D = 1024
FF = 512
EXPERTS = 32
TOP = 8
TOK_DEV = 128
CAP = 36
TOKENS = 2048
N_EXPERT = 4
N_DP = 4


def draw_hidden_in(key, part):
    key = jax.random.fold_in(key, 11)
    row_key, col_key, base_key = jax.random.split(key, 3)
    row_scale = jnp.exp(jax.random.uniform(row_key, (TOKENS, 1), jnp.float32, 0.0, math.log(10.0)))
    col_scale = jnp.exp(jax.random.uniform(col_key, (1, D), jnp.float32, 0.0, math.log(10.0)))
    base_draw = jnp.clip(jax.random.normal(base_key, (TOKENS, D), jnp.float32), -5.0, 5.0)
    return (base_draw * row_scale * col_scale * 0.25).astype(jnp.bfloat16)


def shard_levels(stream_key, shape, cuts, low, top_value):
    def one(axis_at, shards_of):
        heights = jax.random.uniform(jax.random.fold_in(jax.random.fold_in(stream_key, 6), axis_at), (shards_of,), jnp.float32, low / len(cuts), top_value / len(cuts))
        return jnp.repeat(jnp.exp(heights), shape[axis_at] // shards_of).reshape((-1,) + (1,) * (len(shape) - axis_at - 1))

    gain = one(*cuts[0])
    for cut in cuts[1:]:
        gain = gain * one(*cut)
    return gain


def shared_out(own_key, own, number, rows, number_of, top, limit, skew):
    ranking = jax.random.permutation(own_key, number_of)
    crowded, ordinary = load_shares(number_of, rows * top, limit, skew, True), load_shares(number_of, rows * top, limit, skew, False)
    places = jnp.arange(number_of)

    def named(tallies, offset_by):
        used = int((tallies > 0).sum())
        fixed = max(1, used // 4)
        moved = fixed + (places - fixed + offset_by * (used - fixed)) % max(1, number_of - fixed)
        return jnp.zeros((number_of,), jnp.int32).at[ranking[jnp.where(places < fixed, places, moved)]].set(jnp.asarray(tallies, jnp.int32))

    tallies = jnp.where(number % 4 == 0, named(crowded, number // 4), named(ordinary, number - number // 4 - 1))
    mixed = jax.random.permutation(jax.random.fold_in(own, 3), number_of)
    source_of, sink = mixed[0:number_of // 2 * 2:2], mixed[1:number_of // 2 * 2:2]
    slack = jnp.minimum(tallies[source_of] - 1, limit - tallies[sink]) // 2
    slack = jnp.where((source_of == ranking[0]) | (sink == ranking[0]) | (tallies[sink] == 0), 0, jnp.maximum(slack, 0))
    moved = jax.random.randint(jax.random.fold_in(own, 4), (number_of // 2,), 0, 1 << 20) % (slack + 1)
    tallies = tallies.at[source_of].add(-moved).at[sink].add(moved)
    items = jnp.searchsorted(jnp.cumsum(tallies), jnp.arange(rows * top), side="right").astype(jnp.int32)
    grid = items.reshape(top, rows).T
    grid = grid[jax.random.permutation(jax.random.fold_in(own, 1), rows)]
    offset_by = jax.random.randint(jax.random.fold_in(own, 2), (rows, 1), 0, top)
    return jnp.take_along_axis(grid, (jnp.arange(top)[None, :] + offset_by) % top, axis=1)


def load_shares(number_of, total, reach, skew, full):
    portions = [(1 << 20) // math.isqrt(grade ** skew) + 1 for grade in range(1, number_of + 1)]
    largest = reach if full else min(reach, max(-(-total // number_of), total * portions[0] // sum(portions)))
    least = 1 if total - largest >= number_of - 1 else 0
    given, surplus = [largest] + [least] * (number_of - 1), total - largest - least * (number_of - 1)
    while surplus > 0:
        free = [i for i in range(1, number_of) if given[i] < largest] or [i for i in range(1, number_of) if given[i] < reach]
        whole, budget = sum([portions[i] for i in free]), surplus
        for i in free:
            extra = min(reach - given[i], max(1, budget * portions[i] // whole), surplus)
            given[i] = given[i] + extra
            surplus = surplus - extra
    return np.array(given)


def gaussian(own_key, extent, scale, bound, pieces=(), kind=jnp.bfloat16):
    entries = scale * jax.random.normal(own_key, extent, jnp.float32)
    if pieces:
        entries = entries * shard_levels(own_key, extent, pieces, -0.22, 0.18)
    return jnp.clip(entries, -bound, bound).astype(kind)


def setup_inputs(seed: int = 0, part: int = 0) -> dict:
    key_of = jax.random.split(jax.random.key(seed), 10)
    part_splits = jax.random.split(jax.random.fold_in(key_of[9], part), 10)
    hidden_in = draw_hidden_in(jax.random.fold_in(jax.random.fold_in(key_of[9], part), 71), part)
    context = gaussian(part_splits[1], (TOKENS, D), 1.0, 6.0, ((0, 16),))
    norm_gain = jnp.clip(1.0 + 0.18 * jax.random.normal(key_of[2], (D,), jnp.float32), 0.1, 1.9)
    route_ids_keys = jax.random.split(jax.random.fold_in(part_splits[3], 1), TOKENS // TOK_DEV)
    route_ids_turns = jax.random.permutation(jax.random.fold_in(part_splits[3], 3), TOKENS // TOK_DEV)
    route_ids = jax.vmap(lambda own, number: shared_out(jax.random.fold_in(part_splits[3], 2), own, number, TOK_DEV, EXPERTS, TOP, CAP, 2))(route_ids_keys, route_ids_turns).reshape((TOKENS, TOP))
    route_weights = jnp.clip(jnp.exp(math.log(0.4) - 2.5902672 * jax.random.uniform(part_splits[4], (TOKENS, TOP), jnp.float32) ** shard_levels(part_splits[4], (TOKENS, TOP), ((0, 16),), -0.2, 0.2)), 0.03, 0.4)
    w_gate = gaussian(key_of[5], (EXPERTS, D, FF), D ** -0.5, 0.1875, ((0, 4),))
    w_up = gaussian(key_of[6], (EXPERTS, D, FF), D ** -0.5, 0.1875, ((0, 4),))
    w_down = gaussian(key_of[7], (EXPERTS, FF, D), FF ** -0.5, 0.25, ((0, 4),))
    out_grad = gaussian(part_splits[8], (TOKENS, D), 1.0, 6.0, ((0, 16),))
    return dict(hidden_in=hidden_in, context=context, norm_gain=norm_gain, route_ids=route_ids, route_weights=route_weights, w_gate=w_gate, w_up=w_up, w_down=w_down, out_grad=out_grad)


EPSILON = 1e-05

def silu_slope(pre_act):
    sigmoid_val = jax.nn.sigmoid(pre_act)
    return sigmoid_val * (1.0 + pre_act * (1.0 - sigmoid_val))

def expert_pass(packed):
    rows_in, rows_grad, gate_mat, up_mat, down_mat = packed
    flat_in = rows_in.reshape(-1, D)
    flat_grad = rows_grad.reshape(-1, D)
    gate_pre = jnp.dot(flat_in, gate_mat, preferred_element_type=jnp.float32)
    up_pre = jnp.dot(flat_in, up_mat, preferred_element_type=jnp.float32)
    active = jax.nn.silu(gate_pre)
    hidden_act = (active * up_pre).astype(jnp.bfloat16)
    result = jnp.dot(hidden_act, down_mat, preferred_element_type=jnp.float32).astype(jnp.bfloat16)
    inner_grad = jnp.dot(flat_grad, down_mat.T, preferred_element_type=jnp.float32)
    gate_delta = (inner_grad * up_pre * silu_slope(gate_pre)).astype(jnp.bfloat16)
    up_delta = (inner_grad * active).astype(jnp.bfloat16)
    input_delta = (jnp.dot(gate_delta, gate_mat.T, preferred_element_type=jnp.float32) + jnp.dot(up_delta, up_mat.T, preferred_element_type=jnp.float32)).astype(jnp.bfloat16)
    grad_scale = 8.0 / math.sqrt(TOKENS)
    group_in = flat_in.astype(jnp.float32).reshape(N_EXPERT, N_DP, CAP, D)
    group_grad = flat_grad.astype(jnp.float32).reshape(N_EXPERT, N_DP, CAP, D)
    group_act = hidden_act.astype(jnp.float32).reshape(N_EXPERT, N_DP, CAP, FF)
    group_gate = gate_delta.astype(jnp.float32).reshape(N_EXPERT, N_DP, CAP, FF)
    group_up = up_delta.astype(jnp.float32).reshape(N_EXPERT, N_DP, CAP, FF)
    highest = lax.Precision.HIGHEST
    gate_part = jnp.einsum('sgcd,sgcf->gdf', group_in, group_gate, precision=highest) * grad_scale
    up_part = jnp.einsum('sgcd,sgcf->gdf', group_in, group_up, precision=highest) * grad_scale
    down_part = jnp.einsum('sgcf,sgcd->gfd', group_act, group_grad, precision=highest) * grad_scale
    gate_sum = lax.optimization_barrier(jnp.sum(lax.optimization_barrier(gate_part.astype(jnp.bfloat16)).astype(jnp.float32), axis=0))
    up_sum = lax.optimization_barrier(jnp.sum(lax.optimization_barrier(up_part.astype(jnp.bfloat16)).astype(jnp.float32), axis=0))
    down_sum = lax.optimization_barrier(jnp.sum(lax.optimization_barrier(down_part.astype(jnp.bfloat16)).astype(jnp.float32), axis=0))
    return (result.reshape(rows_in.shape), input_delta.reshape(rows_in.shape), gate_sum, up_sum, down_sum)

def reference(hidden_in, context, norm_gain, route_ids, route_weights, w_gate, w_up, w_down, out_grad):
    blocks = TOKENS // TOK_DEV
    per_block = TOK_DEV * TOP
    hidden = hidden_in.astype(jnp.float32)
    inv_rms = lax.rsqrt(lax.optimization_barrier(jnp.mean(hidden * hidden, axis=-1, keepdims=True)) + EPSILON)
    normed = hidden * inv_rms
    scaled_in = (normed * norm_gain).astype(jnp.bfloat16)
    chosen = route_ids.reshape(blocks, per_block).astype(jnp.int32)
    one_hot = (chosen[:, :, None] == jnp.arange(EXPERTS, dtype=jnp.int32)[None, None, :]).astype(jnp.int32)
    earlier = jnp.cumsum(one_hot, axis=1) - one_hot
    position = lax.optimization_barrier(jnp.sum(earlier * one_hot, axis=-1)).astype(jnp.int32)
    target = (chosen * CAP + position).astype(jnp.int32)
    block_row = jnp.arange(blocks, dtype=jnp.int32)[:, None]
    token_of = (block_row * TOK_DEV + jnp.arange(per_block, dtype=jnp.int32)[None, :] // TOP).astype(jnp.int32)
    slot_token = jnp.zeros((blocks, EXPERTS * CAP), jnp.int32).at[block_row, target].set(token_of)
    slot_live = jnp.zeros((blocks, EXPERTS * CAP), jnp.int32).at[block_row, target].set(1)
    slot_weight = jnp.zeros((blocks, EXPERTS * CAP), jnp.float32).at[block_row, target].set(route_weights.reshape(blocks, per_block))
    live_mask = slot_live[..., None] > 0
    out_grad32 = out_grad.astype(jnp.float32)
    send_in = jnp.where(live_mask, scaled_in[slot_token], jnp.zeros((), jnp.bfloat16))
    send_grad = jnp.where(live_mask, (slot_weight[..., None] * out_grad32[slot_token]).astype(jnp.bfloat16), jnp.zeros((), jnp.bfloat16))
    expert_in = send_in.reshape(blocks, EXPERTS, CAP, D).transpose(1, 0, 2, 3)
    expert_grad = send_grad.reshape(blocks, EXPERTS, CAP, D).transpose(1, 0, 2, 3)
    slot_out, slot_delta, gate_grad, up_grad, down_grad = lax.map(expert_pass, (expert_in, expert_grad, w_gate, w_up, w_down))
    back_out = slot_out.transpose(1, 0, 2, 3).reshape(blocks, EXPERTS * CAP, D)
    back_delta = slot_delta.transpose(1, 0, 2, 3).reshape(blocks, EXPERTS * CAP, D)
    take_out = back_out[block_row, target].reshape(TOKENS, TOP, D)
    take_delta = back_delta[block_row, target].reshape(TOKENS, TOP, D)
    moe_out = lax.optimization_barrier(jnp.sum(route_weights[..., None] * take_out.astype(jnp.float32), axis=1)).astype(jnp.bfloat16)
    route_grad = jnp.einsum('tkd,td->tk', take_out.astype(jnp.float32), out_grad32)
    norm_delta = lax.optimization_barrier(jnp.sum(take_delta.astype(jnp.float32), axis=1))
    scaled_delta = norm_delta * norm_gain
    branch = inv_rms * (scaled_delta - normed * lax.optimization_barrier(jnp.mean(scaled_delta * normed, axis=-1, keepdims=True)))
    branch_grad = branch.astype(jnp.bfloat16)
    full_grad = (out_grad32 + branch).astype(jnp.bfloat16)
    proj_grad = jnp.dot(context.T, full_grad, preferred_element_type=jnp.float32) / math.sqrt(TOKENS)
    gain_grad = lax.optimization_barrier(jnp.sum(norm_delta * normed, axis=0)) * (8.0 / math.sqrt(TOKENS))
    return (moe_out, branch_grad, route_grad, gain_grad, proj_grad, gate_grad, up_grad, down_grad)
```

```python
import math

import jax
import jax.numpy as jnp
from jax import lax
from jax.sharding import PartitionSpec as P

EPSILON = 1e-05


def silu_slope(pre_act):
    sigmoid_val = jax.nn.sigmoid(pre_act)
    return sigmoid_val * (1.0 + pre_act * (1.0 - sigmoid_val))


def forward_rows(rows_in, w_gate, w_up, w_down):
    gate_pre = jnp.einsum("sjcd,jdf->sjcf", rows_in, w_gate, preferred_element_type=jnp.float32)
    up_pre = jnp.einsum("sjcd,jdf->sjcf", rows_in, w_up, preferred_element_type=jnp.float32)
    hidden_act = (jax.nn.silu(gate_pre) * up_pre).astype(jnp.bfloat16)
    result = jnp.einsum(
        "sjcf,jfd->sjcd", hidden_act, w_down, preferred_element_type=jnp.float32
    ).astype(jnp.bfloat16)
    return (gate_pre, up_pre, hidden_act, result)


def backward_rows(
    rows_in, gate_pre, up_pre, hidden_act, rows_grad, w_gate, w_up, w_down, grad_scale
):
    inner_grad = jnp.einsum("sjcd,jfd->sjcf", rows_grad, w_down, preferred_element_type=jnp.float32)
    gate_delta = (inner_grad * up_pre * silu_slope(gate_pre)).astype(jnp.bfloat16)
    up_delta = (inner_grad * jax.nn.silu(gate_pre)).astype(jnp.bfloat16)
    input_delta = (
        jnp.einsum("sjcf,jdf->sjcd", gate_delta, w_gate, preferred_element_type=jnp.float32)
        + jnp.einsum("sjcf,jdf->sjcd", up_delta, w_up, preferred_element_type=jnp.float32)
    ).astype(jnp.bfloat16)
    gate_term = (
        jnp.einsum("sjcd,sjcf->jdf", rows_in, gate_delta, preferred_element_type=jnp.float32)
        * grad_scale
    )
    up_term = (
        jnp.einsum("sjcd,sjcf->jdf", rows_in, up_delta, preferred_element_type=jnp.float32)
        * grad_scale
    )
    down_term = (
        jnp.einsum("sjcf,sjcd->jfd", hidden_act, rows_grad, preferred_element_type=jnp.float32)
        * grad_scale
    )
    return (input_delta, gate_term, up_term, down_term)


def scattered_body(hidden_in, context, norm_gain, route_ids, route_weights, w_gate, w_up, w_down, out_grad):
    tok_rows = hidden_in.shape[0]
    feature_count = hidden_in.shape[1]
    top_count = route_ids.shape[1]
    local_experts = w_gate.shape[0]
    owners = lax.axis_size("expert")
    expert_total = local_experts * owners
    capacity = tok_rows * top_count * 9 // (8 * expert_total)
    token_total = tok_rows * owners * lax.axis_size("dp")
    grad_scale = 8.0 / math.sqrt(token_total)
    hidden = hidden_in.astype(jnp.float32)
    inv_rms = lax.rsqrt(jnp.mean(hidden * hidden, axis=-1, keepdims=True) + EPSILON)
    normed = hidden * inv_rms
    scaled_in = (normed * norm_gain).astype(jnp.bfloat16)
    flat_ids = route_ids.reshape(-1)
    one_hot = (flat_ids[:, None] == jnp.arange(expert_total, dtype=jnp.int32)[None, :]).astype(
        jnp.int32
    )
    earlier = jnp.cumsum(one_hot, axis=0) - one_hot
    position = jnp.sum(earlier * one_hot, axis=-1)
    target = flat_ids * capacity + position
    token_of = jnp.arange(tok_rows * top_count, dtype=jnp.int32) // top_count
    slot_token = jnp.zeros((expert_total * capacity,), jnp.int32).at[target].set(token_of)
    slot_live = jnp.zeros((expert_total * capacity,), jnp.int32).at[target].set(1)
    slot_weight = (
        jnp.zeros((expert_total * capacity,), jnp.float32).at[target].set(route_weights.reshape(-1))
    )
    live_mask = slot_live[:, None] > 0
    out_grad32 = out_grad.astype(jnp.float32)
    send_in = jnp.where(live_mask, scaled_in[slot_token], jnp.zeros((), jnp.bfloat16))
    send_grad = jnp.where(
        live_mask,
        (slot_weight[:, None] * out_grad32[slot_token]).astype(jnp.bfloat16),
        jnp.zeros((), jnp.bfloat16),
    )
    buffer_shape = (owners, local_experts, capacity, feature_count)
    send_in = send_in.reshape(buffer_shape)
    send_grad = send_grad.reshape(buffer_shape)
    got_in = lax.all_to_all(send_in, "expert", split_axis=0, concat_axis=0, tiled=True)
    gate_pre, up_pre, hidden_act, result = forward_rows(got_in, w_gate, w_up, w_down)
    back_out = lax.all_to_all(result, "expert", split_axis=0, concat_axis=0, tiled=True)
    got_grad = lax.all_to_all(send_grad, "expert", split_axis=0, concat_axis=0, tiled=True)
    input_delta, gate_term, up_term, down_term = backward_rows(
        got_in, gate_pre, up_pre, hidden_act, got_grad, w_gate, w_up, w_down, grad_scale
    )
    back_delta = lax.all_to_all(input_delta, "expert", split_axis=0, concat_axis=0, tiled=True)
    gate_grad, up_grad, down_grad = (
        lax.psum_scatter(
            gate_term.astype(jnp.bfloat16), "dp", scatter_dimension=1, tiled=True
        ).astype(jnp.float32),
        lax.psum_scatter(
            up_term.astype(jnp.bfloat16), "dp", scatter_dimension=1, tiled=True
        ).astype(jnp.float32),
        lax.psum_scatter(
            down_term.astype(jnp.bfloat16), "dp", scatter_dimension=1, tiled=True
        ).astype(jnp.float32),
    )
    take_out = back_out.reshape(expert_total * capacity, feature_count)[target].reshape(
        tok_rows, top_count, feature_count
    )
    take_delta = back_delta.reshape(expert_total * capacity, feature_count)[target].reshape(
        tok_rows, top_count, feature_count
    )
    moe_out = jnp.sum(route_weights[..., None] * take_out.astype(jnp.float32), axis=1).astype(
        jnp.bfloat16
    )
    route_grad = jnp.einsum("tkd,td->tk", take_out, out_grad, preferred_element_type=jnp.float32)
    norm_delta = jnp.sum(take_delta.astype(jnp.float32), axis=1)
    scaled_delta = norm_delta * norm_gain
    branch = inv_rms * (
        scaled_delta - normed * jnp.mean(scaled_delta * normed, axis=-1, keepdims=True)
    )
    branch_grad = branch.astype(jnp.bfloat16)
    full_grad = (out_grad32 + branch).astype(jnp.bfloat16)
    proj_term = lax.dot_general(
        context, full_grad, (((0,), (0,)), ((), ())), preferred_element_type=jnp.float32
    ) / math.sqrt(token_total)
    gain_term = jnp.sum(norm_delta * normed, axis=0) * grad_scale
    proj_grad, gain_grad = (
        lax.psum_scatter(proj_term, ("expert", "dp"), scatter_dimension=0, tiled=True),
        lax.psum_scatter(gain_term, ("expert", "dp"), scatter_dimension=0, tiled=True),
    )
    return (moe_out, branch_grad, route_grad, gain_grad, proj_grad, gate_grad, up_grad, down_grad)


def token_rows(ids, local_experts, capacity, first_expert):
    blocks, owners, tok_rows, _ = ids.shape
    named = first_expert + jnp.arange(local_experts, dtype=jnp.int32)
    hit = jnp.any(ids[..., None] == named, axis=3)
    order = jnp.arange(tok_rows)
    before = (order[:, None] > order[None, :]).astype(jnp.bfloat16)
    position = jnp.einsum(
        "ut,sbtj->sbuj", before, hit.astype(jnp.bfloat16), preferred_element_type=jnp.float32
    ).astype(jnp.int32)
    base = jnp.arange(owners, dtype=jnp.int32)[None, :, None, None] * capacity
    row = jnp.where(hit, base + position, -1)
    return row.reshape(blocks, owners * tok_rows, local_experts)


def gathered_body(hidden_in, context, norm_gain, route_ids, route_weights, w_gate, w_up, w_down, out_grad):
    tok_rows, feature_count = hidden_in.shape
    top_count = route_ids.shape[1]
    local_experts, _, hidden_units = w_gate.shape
    owners, parts = lax.axis_size("expert"), lax.axis_size("dp")
    expert_at, part_at = lax.axis_index("expert"), lax.axis_index("dp")
    capacity = tok_rows * top_count * 9 // (8 * local_experts * owners)
    token_total = tok_rows * owners * parts
    grad_scale = 8.0 / math.sqrt(token_total)
    super_toks, super_rows = owners * tok_rows, owners * capacity
    hidden = hidden_in.astype(jnp.float32)
    inv_rms = lax.rsqrt(jnp.mean(hidden * hidden, axis=-1, keepdims=True) + EPSILON)
    normed = hidden * inv_rms
    scaled_in = (normed * norm_gain).astype(jnp.bfloat16)

    def everywhere(block):
        got = lax.all_gather(block, ("dp", "expert"), axis=0, tiled=True)
        return got.reshape(parts, super_toks, block.shape[1])

    routes = everywhere(jnp.concatenate([route_ids.astype(jnp.float32), route_weights], axis=1))
    tok_in = everywhere(scaled_in)
    tok_grad = everywhere(out_grad)
    ids = routes[..., :top_count].astype(jnp.int32)
    weights = routes[..., top_count:]
    first_expert = expert_at * local_experts
    row = token_rows(
        ids.reshape(parts, owners, tok_rows, top_count), local_experts, capacity, first_expert
    )
    named = first_expert + jnp.arange(local_experts, dtype=jnp.int32)
    match = ids[..., None] == named
    tok_weight = jnp.sum(jnp.where(match, weights[..., None], 0.0), axis=2)
    slots = jnp.arange(super_rows, dtype=jnp.int32)
    pick_mask = row.transpose(2, 0, 1)[:, :, None, :] == slots[:, None]
    pick = pick_mask.astype(jnp.bfloat16)
    slot_weight = jnp.sum(
        jnp.where(pick_mask, tok_weight.transpose(2, 0, 1)[:, :, None, :], 0.0), axis=-1
    )
    rows_in = jnp.einsum(
        "jsct,std->jscd", pick, tok_in, preferred_element_type=jnp.float32
    ).astype(jnp.bfloat16)
    raw_grad = jnp.einsum("jsct,std->jscd", pick, tok_grad, preferred_element_type=jnp.float32)
    rows_grad = (slot_weight[..., None] * raw_grad).astype(jnp.bfloat16)
    flat = (local_experts, parts * super_rows)
    rows_in = rows_in.reshape(*flat, feature_count)
    rows_grad = rows_grad.reshape(*flat, feature_count)
    dot = lambda spec, a, b: jnp.einsum(spec, a, b, preferred_element_type=jnp.float32)
    gate_pre = dot("jrd,jdf->jrf", rows_in, w_gate)
    up_pre = dot("jrd,jdf->jrf", rows_in, w_up)
    hidden_act = (jax.nn.silu(gate_pre) * up_pre).astype(jnp.bfloat16)
    inner_grad = dot("jrd,jfd->jrf", rows_grad, w_down)
    gate_delta = (inner_grad * up_pre * silu_slope(gate_pre)).astype(jnp.bfloat16)
    up_delta = (inner_grad * jax.nn.silu(gate_pre)).astype(jnp.bfloat16)

    def own(rows):
        return lax.dynamic_slice_in_dim(rows, part_at * super_rows, super_rows, axis=1)

    own_pick = lax.dynamic_index_in_dim(pick, part_at, axis=1, keepdims=False)
    own_weight = lax.dynamic_index_in_dim(tok_weight, part_at, axis=0, keepdims=False)
    own_match = lax.dynamic_index_in_dim(match, part_at, axis=0, keepdims=False)
    own_raw = lax.dynamic_index_in_dim(raw_grad, part_at, axis=1, keepdims=False)
    result = dot("jcf,jfd->jcd", own(hidden_act), w_down).astype(jnp.bfloat16)
    input_delta = (
        dot("jcf,jdf->jcd", own(gate_delta), w_gate) + dot("jcf,jdf->jcd", own(up_delta), w_up)
    ).astype(jnp.bfloat16)
    weighted = own_pick * own_weight.T.astype(jnp.bfloat16)[:, None, :]
    moe_term = dot("jct,jcd->td", weighted, result).astype(jnp.bfloat16)
    delta_term = dot("jct,jcd->td", own_pick, input_delta).astype(jnp.bfloat16)
    slot_route = jnp.sum(own_raw * result.astype(jnp.float32), axis=-1)
    tok_route = jnp.sum(jnp.where(own_pick > 0, slot_route[..., None], 0.0), axis=1)
    route_term = jnp.sum(jnp.where(own_match, tok_route.T[:, None, :], 0.0), axis=-1)
    scatter = lambda term: lax.psum_scatter(term, "expert", scatter_dimension=0, tiled=True)
    moe_out = scatter(moe_term)
    norm_delta = scatter(delta_term).astype(jnp.float32)
    route_grad = scatter(route_term)

    cols, units = feature_count // parts, hidden_units // parts
    cut_in = lax.dynamic_slice_in_dim(rows_in, part_at * cols, cols, axis=2)
    cut_act = lax.dynamic_slice_in_dim(hidden_act, part_at * units, units, axis=2)
    gate_grad = dot("jrd,jrf->jdf", cut_in, gate_delta) * grad_scale
    up_grad = dot("jrd,jrf->jdf", cut_in, up_delta) * grad_scale
    down_grad = dot("jrf,jrd->jfd", cut_act, rows_grad) * grad_scale

    scaled_delta = norm_delta * norm_gain
    branch = inv_rms * (
        scaled_delta - normed * jnp.mean(scaled_delta * normed, axis=-1, keepdims=True)
    )
    branch_grad = branch.astype(jnp.bfloat16)
    full_grad = (out_grad.astype(jnp.float32) + branch).astype(jnp.bfloat16)
    proj_term = lax.dot_general(
        context, full_grad, (((0,), (0,)), ((), ())), preferred_element_type=jnp.float32
    ) / math.sqrt(token_total)
    gain_term = jnp.sum(norm_delta * normed, axis=0) * grad_scale
    everyone = lambda term: lax.psum_scatter(
        term, ("expert", "dp"), scatter_dimension=0, tiled=True
    )
    proj_grad = everyone(proj_term.astype(jnp.bfloat16)).astype(jnp.float32)
    gain_grad = everyone(gain_term)
    return (moe_out, branch_grad, route_grad, gain_grad, proj_grad, gate_grad, up_grad, down_grad)


def body(*args):
    few = lax.axis_size("dp") <= 4 and lax.axis_size("expert") <= 4
    return (gathered_body if few else scattered_body)(*args)


def solution(mesh):
    return jax.shard_map(
        body,
        mesh=mesh,
        in_specs=(
            P(("groups", "expert", "dp"), None),
            P(("groups", "expert", "dp"), None),
            P(),
            P(("groups", "expert", "dp"), None),
            P(("groups", "expert", "dp"), None),
            P("expert", None, None),
            P("expert", None, None),
            P("expert", None, None),
            P(("groups", "expert", "dp"), None),
        ),
        out_specs=(
            P(("groups", "expert", "dp"), None),
            P(("groups", "expert", "dp"), None),
            P(("groups", "expert", "dp"), None),
            P(("groups", "expert", "dp")),
            P(("groups", "expert", "dp"), None),
            P(("groups", "expert"), "dp", None),
            P(("groups", "expert"), "dp", None),
            P(("groups", "expert"), "dp", None),
        ),
        check_vma=False,
    )
```

```python
import math

import jax
import jax.numpy as jnp
from jax import lax
from jax.experimental import pallas as pl
from jax.experimental.pallas import tpu as pltpu
from jax.sharding import PartitionSpec as P

EPSILON = 1e-05


def silu_slope(pre_act):
    sigmoid_val = jax.nn.sigmoid(pre_act)
    return sigmoid_val * (1.0 + pre_act * (1.0 - sigmoid_val))


def forward_rows(rows_in, w_gate, w_up, w_down):
    gate_pre = jnp.einsum("sjcd,jdf->sjcf", rows_in, w_gate, preferred_element_type=jnp.float32)
    up_pre = jnp.einsum("sjcd,jdf->sjcf", rows_in, w_up, preferred_element_type=jnp.float32)
    hidden_act = (jax.nn.silu(gate_pre) * up_pre).astype(jnp.bfloat16)
    result = jnp.einsum(
        "sjcf,jfd->sjcd", hidden_act, w_down, preferred_element_type=jnp.float32
    ).astype(jnp.bfloat16)
    return (gate_pre, up_pre, hidden_act, result)


def backward_rows(
    rows_in, gate_pre, up_pre, hidden_act, rows_grad, w_gate, w_up, w_down, grad_scale
):
    inner_grad = jnp.einsum("sjcd,jfd->sjcf", rows_grad, w_down, preferred_element_type=jnp.float32)
    gate_delta = (inner_grad * up_pre * silu_slope(gate_pre)).astype(jnp.bfloat16)
    up_delta = (inner_grad * jax.nn.silu(gate_pre)).astype(jnp.bfloat16)
    input_delta = (
        jnp.einsum("sjcf,jdf->sjcd", gate_delta, w_gate, preferred_element_type=jnp.float32)
        + jnp.einsum("sjcf,jdf->sjcd", up_delta, w_up, preferred_element_type=jnp.float32)
    ).astype(jnp.bfloat16)
    gate_term = (
        jnp.einsum("sjcd,sjcf->jdf", rows_in, gate_delta, preferred_element_type=jnp.float32)
        * grad_scale
    )
    up_term = (
        jnp.einsum("sjcd,sjcf->jdf", rows_in, up_delta, preferred_element_type=jnp.float32)
        * grad_scale
    )
    down_term = (
        jnp.einsum("sjcf,sjcd->jfd", hidden_act, rows_grad, preferred_element_type=jnp.float32)
        * grad_scale
    )
    return (input_delta, gate_term, up_term, down_term)


def scattered_body(hidden_in, context, norm_gain, route_ids, route_weights, w_gate, w_up, w_down, out_grad):
    tok_rows = hidden_in.shape[0]
    feature_count = hidden_in.shape[1]
    top_count = route_ids.shape[1]
    local_experts = w_gate.shape[0]
    owners = lax.axis_size("expert")
    expert_total = local_experts * owners
    capacity = tok_rows * top_count * 9 // (8 * expert_total)
    token_total = tok_rows * owners * lax.axis_size("dp")
    grad_scale = 8.0 / math.sqrt(token_total)
    hidden = hidden_in.astype(jnp.float32)
    inv_rms = lax.rsqrt(jnp.mean(hidden * hidden, axis=-1, keepdims=True) + EPSILON)
    normed = hidden * inv_rms
    scaled_in = (normed * norm_gain).astype(jnp.bfloat16)
    flat_ids = route_ids.reshape(-1)
    one_hot = (flat_ids[:, None] == jnp.arange(expert_total, dtype=jnp.int32)[None, :]).astype(
        jnp.int32
    )
    earlier = jnp.cumsum(one_hot, axis=0) - one_hot
    position = jnp.sum(earlier * one_hot, axis=-1)
    target = flat_ids * capacity + position
    token_of = jnp.arange(tok_rows * top_count, dtype=jnp.int32) // top_count
    slot_token = jnp.zeros((expert_total * capacity,), jnp.int32).at[target].set(token_of)
    slot_live = jnp.zeros((expert_total * capacity,), jnp.int32).at[target].set(1)
    slot_weight = (
        jnp.zeros((expert_total * capacity,), jnp.float32).at[target].set(route_weights.reshape(-1))
    )
    live_mask = slot_live[:, None] > 0
    out_grad32 = out_grad.astype(jnp.float32)
    send_in = jnp.where(live_mask, scaled_in[slot_token], jnp.zeros((), jnp.bfloat16))
    send_grad = jnp.where(
        live_mask,
        (slot_weight[:, None] * out_grad32[slot_token]).astype(jnp.bfloat16),
        jnp.zeros((), jnp.bfloat16),
    )
    buffer_shape = (owners, local_experts, capacity, feature_count)
    send_in = send_in.reshape(buffer_shape)
    send_grad = send_grad.reshape(buffer_shape)
    got_in = lax.all_to_all(send_in, "expert", split_axis=0, concat_axis=0, tiled=True)
    gate_pre, up_pre, hidden_act, result = forward_rows(got_in, w_gate, w_up, w_down)
    back_out = lax.all_to_all(result, "expert", split_axis=0, concat_axis=0, tiled=True)
    got_grad = lax.all_to_all(send_grad, "expert", split_axis=0, concat_axis=0, tiled=True)
    input_delta, gate_term, up_term, down_term = backward_rows(
        got_in, gate_pre, up_pre, hidden_act, got_grad, w_gate, w_up, w_down, grad_scale
    )
    back_delta = lax.all_to_all(input_delta, "expert", split_axis=0, concat_axis=0, tiled=True)
    gate_grad, up_grad, down_grad = (
        lax.psum_scatter(
            gate_term.astype(jnp.bfloat16), "dp", scatter_dimension=1, tiled=True
        ).astype(jnp.float32),
        lax.psum_scatter(
            up_term.astype(jnp.bfloat16), "dp", scatter_dimension=1, tiled=True
        ).astype(jnp.float32),
        lax.psum_scatter(
            down_term.astype(jnp.bfloat16), "dp", scatter_dimension=1, tiled=True
        ).astype(jnp.float32),
    )
    take_out = back_out.reshape(expert_total * capacity, feature_count)[target].reshape(
        tok_rows, top_count, feature_count
    )
    take_delta = back_delta.reshape(expert_total * capacity, feature_count)[target].reshape(
        tok_rows, top_count, feature_count
    )
    moe_out = jnp.sum(route_weights[..., None] * take_out.astype(jnp.float32), axis=1).astype(
        jnp.bfloat16
    )
    route_grad = jnp.einsum("tkd,td->tk", take_out, out_grad, preferred_element_type=jnp.float32)
    norm_delta = jnp.sum(take_delta.astype(jnp.float32), axis=1)
    scaled_delta = norm_delta * norm_gain
    branch = inv_rms * (
        scaled_delta - normed * jnp.mean(scaled_delta * normed, axis=-1, keepdims=True)
    )
    branch_grad = branch.astype(jnp.bfloat16)
    full_grad = (out_grad32 + branch).astype(jnp.bfloat16)
    proj_term = lax.dot_general(
        context, full_grad, (((0,), (0,)), ((), ())), preferred_element_type=jnp.float32
    ) / math.sqrt(token_total)
    gain_term = jnp.sum(norm_delta * normed, axis=0) * grad_scale
    proj_grad, gain_grad = (
        lax.psum_scatter(proj_term, ("expert", "dp"), scatter_dimension=0, tiled=True),
        lax.psum_scatter(gain_term, ("expert", "dp"), scatter_dimension=0, tiled=True),
    )
    return (moe_out, branch_grad, route_grad, gain_grad, proj_grad, gate_grad, up_grad, down_grad)


def spread_kernel(a_in, b_in, a_all, b_all, own_sem, send_sem, recv_sem):
    parts, owners = a_all.shape[:2]
    at, line = lax.axis_index("expert"), lax.axis_index("dp")
    sibling = at + 1 - 2 * lax.rem(at, 2)
    across = lax.rem(at + 2, owners)
    sibling_across = lax.rem(sibling + 2, owners)
    below, above = line > 0, line < parts - 1
    always = line >= 0
    partner = {
        "across": (across, line, always),
        "above": (at, line + 1, above),
        "below": (at, line - 1, below),
        "sibling": (sibling, line, always),
    }
    names = list(partner)
    barrier = pltpu.get_barrier_semaphore()
    for name in names:
        to, to_line, cond = partner[name]

        @pl.when(cond)
        def _():
            pl.semaphore_signal(
                barrier,
                inc=1,
                device_id={"expert": to, "dp": to_line},
                device_id_type=pl.DeviceIdType.MESH,
            )

    neighbours = lax.div(line + parts - 1, parts) + lax.div(2 * parts - 2 - line, parts)
    pl.semaphore_wait(barrier, 2 + neighbours)

    buffers = (a_all, b_all)
    started = []

    def copy(which, of, of_line, name, source):
        to, to_line, _ = partner[name]
        place = buffers[which].at[of_line, of]
        return pltpu.make_async_remote_copy(
            src_ref=place if source is None else source,
            dst_ref=place,
            send_sem=send_sem.at[which, of_line, of, names.index(name)],
            recv_sem=recv_sem.at[which, of_line, of],
            device_id={"expert": to, "dp": to_line},
            device_id_type=pl.DeviceIdType.MESH,
        )

    def push(which, of, of_line, there, name, source=None):
        cond = jnp.logical_and(there, partner[name][2])

        @pl.when(cond)
        def _():
            copy(which, of, of_line, name, source).start()

        started.append((which, of, of_line, cond, name, source))

    def arrived(which, of, of_line, there):
        @pl.when(there)
        def _():
            copy(which, of, of_line, "sibling", None).wait_recv()

    def relay(which, of, of_line, there, targets):
        arrived(which, of, of_line, there)
        for name in targets:
            push(which, of, of_line, there, name)

    mine = [
        pltpu.make_async_copy(source, buffer.at[line, at], own_sem.at[i])
        for i, (source, buffer) in enumerate(((a_in, a_all), (b_in, b_all)))
    ]
    for name in ("above", "below", "across", "sibling"):
        push(0, at, line, always, name, a_in)
        push(1, at, line, always, name, b_in)
    for copy_in in mine:
        copy_in.start()
    for step in range(1, parts + 1):
        low, high = line - step, line + step
        has_low, has_high = low >= 0, high < parts
        low1, high1 = line - (step - 1), line + (step - 1)
        has_low1, has_high1 = low1 >= 0, high1 < parts
        if step < parts:
            relay(0, at, low, has_low, ("above", "across", "sibling"))
            relay(0, at, high, has_high, ("below", "across", "sibling"))
        if step == 1:
            relay(1, across, line, always, ("above", "below", "sibling"))
        else:
            relay(1, across, low1, has_low1, ("above", "sibling"))
            relay(1, across, high1, has_high1, ("below", "sibling"))
        if step < parts:
            relay(1, at, low, has_low, ("above", "sibling"))
            relay(1, at, high, has_high, ("below", "sibling"))
        if step == 1:
            relay(0, across, line, always, ("sibling",))
        else:
            relay(0, across, low1, has_low1, ("sibling",))
            relay(0, across, high1, has_high1, ("sibling",))
    for of_line in range(parts):
        for of in (sibling, sibling_across):
            for which in range(2):
                arrived(which, of, of_line, always)
    for which, of, of_line, cond, name, source in started:

        @pl.when(cond)
        def _():
            copy(which, of, of_line, name, source).wait_send()

    for copy_in in mine:
        copy_in.wait()


def spread(a_block, b_block, parts, owners):
    any_space = pl.BlockSpec(memory_space=pl.ANY)
    return pl.pallas_call(
        spread_kernel,
        out_shape=[
            jax.ShapeDtypeStruct((parts, owners, *block.shape), block.dtype)
            for block in (a_block, b_block)
        ],
        in_specs=[any_space, any_space],
        out_specs=[any_space, any_space],
        scratch_shapes=[
            pltpu.SemaphoreType.DMA((2,)),
            pltpu.SemaphoreType.DMA((2, parts, owners, 4)),
            pltpu.SemaphoreType.DMA((2, parts, owners)),
        ],
        compiler_params=pltpu.CompilerParams(collective_id=0, has_side_effects=True),
    )(a_block, b_block)


def three_terms(value):
    high = lax.reduce_precision(value, 8, 7)
    middle = lax.reduce_precision(value - high, 8, 7)
    low = value - high - middle
    return [term.astype(jnp.bfloat16) for term in (high, middle, low)]


def token_rows(ids, local_experts, capacity, first_expert):
    blocks, owners, tok_rows, _ = ids.shape
    named = first_expert + jnp.arange(local_experts, dtype=jnp.int32)
    hit = jnp.any(ids[..., None] == named, axis=3)
    order = jnp.arange(tok_rows)
    before = (order[:, None] > order[None, :]).astype(jnp.bfloat16)
    position = jnp.einsum(
        "ut,sbtj->sbuj", before, hit.astype(jnp.bfloat16), preferred_element_type=jnp.float32
    ).astype(jnp.int32)
    base = jnp.arange(owners, dtype=jnp.int32)[None, :, None, None] * capacity
    row = jnp.where(hit, base + position, -1)
    return row.reshape(blocks, owners * tok_rows, local_experts)


def gathered_body(hidden_in, context, norm_gain, route_ids, route_weights, w_gate, w_up, w_down, out_grad):
    tok_rows, feature_count = hidden_in.shape
    top_count = route_ids.shape[1]
    local_experts, _, hidden_units = w_gate.shape
    owners, parts = lax.axis_size("expert"), lax.axis_size("dp")
    expert_at, part_at = lax.axis_index("expert"), lax.axis_index("dp")
    capacity = tok_rows * top_count * 9 // (8 * local_experts * owners)
    token_total = tok_rows * owners * parts
    grad_scale = 8.0 / math.sqrt(token_total)
    super_toks, super_rows = owners * tok_rows, owners * capacity
    hidden = hidden_in.astype(jnp.float32)
    inv_rms = lax.rsqrt(jnp.mean(hidden * hidden, axis=-1, keepdims=True) + EPSILON)
    normed = hidden * inv_rms
    scaled_in = (normed * norm_gain).astype(jnp.bfloat16)

    routes = jnp.concatenate([route_ids.astype(jnp.bfloat16), *three_terms(route_weights)], axis=1)
    routes = jnp.pad(routes, ((0, 0), (0, -routes.shape[1] % 128)))
    tok_in, tok_grad = spread(
        jnp.concatenate([scaled_in, routes], axis=1), out_grad, parts, owners
    )
    tok_in = tok_in.reshape(parts, super_toks, -1)
    tok_grad = tok_grad.reshape(parts, super_toks, feature_count)
    routes = tok_in[..., feature_count:].astype(jnp.float32)
    tok_in = tok_in[..., :feature_count]
    terms = [routes[..., i * top_count : (i + 1) * top_count] for i in range(4)]
    ids = terms[0].astype(jnp.int32)
    weights = terms[1] + terms[2] + terms[3]
    first_expert = expert_at * local_experts
    row = token_rows(
        ids.reshape(parts, owners, tok_rows, top_count), local_experts, capacity, first_expert
    )
    named = first_expert + jnp.arange(local_experts, dtype=jnp.int32)
    match = ids[..., None] == named
    tok_weight = jnp.sum(jnp.where(match, weights[..., None], 0.0), axis=2)
    slots = jnp.arange(super_rows, dtype=jnp.int32)
    pick_mask = row.transpose(2, 0, 1)[:, :, None, :] == slots[:, None]
    pick = pick_mask.astype(jnp.bfloat16)
    slot_weight = jnp.sum(
        jnp.where(pick_mask, tok_weight.transpose(2, 0, 1)[:, :, None, :], 0.0), axis=-1
    )
    rows_in = jnp.einsum(
        "jsct,std->jscd", pick, tok_in, preferred_element_type=jnp.float32
    ).astype(jnp.bfloat16)
    raw_grad = jnp.einsum("jsct,std->jscd", pick, tok_grad, preferred_element_type=jnp.float32)
    rows_grad = (slot_weight[..., None] * raw_grad).astype(jnp.bfloat16)
    flat = (local_experts, parts * super_rows)
    rows_in = rows_in.reshape(*flat, feature_count)
    rows_grad = rows_grad.reshape(*flat, feature_count)
    dot = lambda spec, a, b: jnp.einsum(spec, a, b, preferred_element_type=jnp.float32)
    gate_pre = dot("jrd,jdf->jrf", rows_in, w_gate)
    up_pre = dot("jrd,jdf->jrf", rows_in, w_up)
    hidden_act = (jax.nn.silu(gate_pre) * up_pre).astype(jnp.bfloat16)
    inner_grad = dot("jrd,jfd->jrf", rows_grad, w_down)
    gate_delta = (inner_grad * up_pre * silu_slope(gate_pre)).astype(jnp.bfloat16)
    up_delta = (inner_grad * jax.nn.silu(gate_pre)).astype(jnp.bfloat16)

    def own(rows):
        return lax.dynamic_slice_in_dim(rows, part_at * super_rows, super_rows, axis=1)

    own_pick = lax.dynamic_index_in_dim(pick, part_at, axis=1, keepdims=False)
    own_weight = lax.dynamic_index_in_dim(tok_weight, part_at, axis=0, keepdims=False)
    own_match = lax.dynamic_index_in_dim(match, part_at, axis=0, keepdims=False)
    own_raw = lax.dynamic_index_in_dim(raw_grad, part_at, axis=1, keepdims=False)
    result = dot("jcf,jfd->jcd", own(hidden_act), w_down).astype(jnp.bfloat16)
    input_delta = (
        dot("jcf,jdf->jcd", own(gate_delta), w_gate) + dot("jcf,jdf->jcd", own(up_delta), w_up)
    ).astype(jnp.bfloat16)
    weighted = own_pick * own_weight.T.astype(jnp.bfloat16)[:, None, :]
    moe_term = dot("jct,jcd->td", weighted, result).astype(jnp.bfloat16)
    delta_term = dot("jct,jcd->td", own_pick, input_delta).astype(jnp.bfloat16)
    slot_route = jnp.sum(own_raw * result.astype(jnp.float32), axis=-1)
    tok_route = jnp.sum(jnp.where(own_pick > 0, slot_route[..., None], 0.0), axis=1)
    route_term = jnp.sum(jnp.where(own_match, tok_route.T[:, None, :], 0.0), axis=-1)

    def scatter(term):
        cut = term.reshape(owners, tok_rows, -1)
        got = lax.all_to_all(cut, "expert", split_axis=0, concat_axis=0, tiled=True)
        return jnp.sum(got.astype(jnp.float32), axis=0)

    norm_delta = scatter(delta_term)
    moe_out = scatter(moe_term).astype(jnp.bfloat16)
    route_grad = scatter(route_term)

    cols, units = feature_count // parts, hidden_units // parts
    cut_in = lax.dynamic_slice_in_dim(rows_in, part_at * cols, cols, axis=2)
    cut_act = lax.dynamic_slice_in_dim(hidden_act, part_at * units, units, axis=2)
    gate_grad = dot("jrd,jrf->jdf", cut_in, gate_delta) * grad_scale
    up_grad = dot("jrd,jrf->jdf", cut_in, up_delta) * grad_scale
    down_grad = dot("jrf,jrd->jfd", cut_act, rows_grad) * grad_scale

    scaled_delta = norm_delta * norm_gain
    branch = inv_rms * (
        scaled_delta - normed * jnp.mean(scaled_delta * normed, axis=-1, keepdims=True)
    )
    branch_grad = branch.astype(jnp.bfloat16)
    full_grad = (out_grad.astype(jnp.float32) + branch).astype(jnp.bfloat16)
    proj_term = lax.dot_general(
        context, full_grad, (((0,), (0,)), ((), ())), preferred_element_type=jnp.float32
    ) / math.sqrt(token_total)
    gain_term = jnp.sum(norm_delta * normed, axis=0) * grad_scale
    gain_cols = jnp.stack(three_terms(gain_term), axis=1)
    gain_cols = jnp.pad(gain_cols, ((0, 0), (0, 125)))
    both = jnp.concatenate([proj_term.astype(jnp.bfloat16), gain_cols], axis=1)
    both = lax.psum_scatter(both, ("expert", "dp"), scatter_dimension=0, tiled=True)
    both = both.astype(jnp.float32)
    proj_grad = both[:, :feature_count]
    gain_grad = jnp.sum(both[:, feature_count:], axis=1)
    return (moe_out, branch_grad, route_grad, gain_grad, proj_grad, gate_grad, up_grad, down_grad)


def body(*args):
    few = lax.axis_size("dp") <= 4 and lax.axis_size("expert") == 4
    return (gathered_body if few else scattered_body)(*args)


def solution(mesh):
    return jax.shard_map(
        body,
        mesh=mesh,
        in_specs=(
            P(("groups", "expert", "dp"), None),
            P(("groups", "expert", "dp"), None),
            P(),
            P(("groups", "expert", "dp"), None),
            P(("groups", "expert", "dp"), None),
            P("expert", None, None),
            P("expert", None, None),
            P("expert", None, None),
            P(("groups", "expert", "dp"), None),
        ),
        out_specs=(
            P(("groups", "expert", "dp"), None),
            P(("groups", "expert", "dp"), None),
            P(("groups", "expert", "dp"), None),
            P(("groups", "expert", "dp")),
            P(("groups", "expert", "dp"), None),
            P(("groups", "expert"), "dp", None),
            P(("groups", "expert"), "dp", None),
            P(("groups", "expert"), "dp", None),
        ),
        check_vma=False,
    )
```

```python
import functools
import math

import jax
import jax.numpy as jnp
from jax import lax
from jax.experimental import pallas as pl
from jax.experimental.pallas import tpu as pltpu
from jax.sharding import PartitionSpec as P

EPSILON = 1e-05


def silu_slope(pre_act):
    sigmoid_val = jax.nn.sigmoid(pre_act)
    return sigmoid_val * (1.0 + pre_act * (1.0 - sigmoid_val))


def forward_rows(rows_in, w_gate, w_up, w_down):
    gate_pre = jnp.einsum("sjcd,jdf->sjcf", rows_in, w_gate, preferred_element_type=jnp.float32)
    up_pre = jnp.einsum("sjcd,jdf->sjcf", rows_in, w_up, preferred_element_type=jnp.float32)
    hidden_act = (jax.nn.silu(gate_pre) * up_pre).astype(jnp.bfloat16)
    result = jnp.einsum(
        "sjcf,jfd->sjcd", hidden_act, w_down, preferred_element_type=jnp.float32
    ).astype(jnp.bfloat16)
    return (gate_pre, up_pre, hidden_act, result)


def backward_rows(
    rows_in, gate_pre, up_pre, hidden_act, rows_grad, w_gate, w_up, w_down, grad_scale
):
    inner_grad = jnp.einsum("sjcd,jfd->sjcf", rows_grad, w_down, preferred_element_type=jnp.float32)
    gate_delta = (inner_grad * up_pre * silu_slope(gate_pre)).astype(jnp.bfloat16)
    up_delta = (inner_grad * jax.nn.silu(gate_pre)).astype(jnp.bfloat16)
    input_delta = (
        jnp.einsum("sjcf,jdf->sjcd", gate_delta, w_gate, preferred_element_type=jnp.float32)
        + jnp.einsum("sjcf,jdf->sjcd", up_delta, w_up, preferred_element_type=jnp.float32)
    ).astype(jnp.bfloat16)
    gate_term = (
        jnp.einsum("sjcd,sjcf->jdf", rows_in, gate_delta, preferred_element_type=jnp.float32)
        * grad_scale
    )
    up_term = (
        jnp.einsum("sjcd,sjcf->jdf", rows_in, up_delta, preferred_element_type=jnp.float32)
        * grad_scale
    )
    down_term = (
        jnp.einsum("sjcf,sjcd->jfd", hidden_act, rows_grad, preferred_element_type=jnp.float32)
        * grad_scale
    )
    return (input_delta, gate_term, up_term, down_term)


def scattered_body(hidden_in, context, norm_gain, route_ids, route_weights, w_gate, w_up, w_down, out_grad):
    tok_rows = hidden_in.shape[0]
    feature_count = hidden_in.shape[1]
    top_count = route_ids.shape[1]
    local_experts = w_gate.shape[0]
    owners = lax.axis_size("expert")
    expert_total = local_experts * owners
    capacity = tok_rows * top_count * 9 // (8 * expert_total)
    token_total = tok_rows * owners * lax.axis_size("dp")
    grad_scale = 8.0 / math.sqrt(token_total)
    hidden = hidden_in.astype(jnp.float32)
    inv_rms = lax.rsqrt(jnp.mean(hidden * hidden, axis=-1, keepdims=True) + EPSILON)
    normed = hidden * inv_rms
    scaled_in = (normed * norm_gain).astype(jnp.bfloat16)
    flat_ids = route_ids.reshape(-1)
    one_hot = (flat_ids[:, None] == jnp.arange(expert_total, dtype=jnp.int32)[None, :]).astype(
        jnp.int32
    )
    earlier = jnp.cumsum(one_hot, axis=0) - one_hot
    position = jnp.sum(earlier * one_hot, axis=-1)
    target = flat_ids * capacity + position
    token_of = jnp.arange(tok_rows * top_count, dtype=jnp.int32) // top_count
    slot_token = jnp.zeros((expert_total * capacity,), jnp.int32).at[target].set(token_of)
    slot_live = jnp.zeros((expert_total * capacity,), jnp.int32).at[target].set(1)
    slot_weight = (
        jnp.zeros((expert_total * capacity,), jnp.float32).at[target].set(route_weights.reshape(-1))
    )
    live_mask = slot_live[:, None] > 0
    out_grad32 = out_grad.astype(jnp.float32)
    send_in = jnp.where(live_mask, scaled_in[slot_token], jnp.zeros((), jnp.bfloat16))
    send_grad = jnp.where(
        live_mask,
        (slot_weight[:, None] * out_grad32[slot_token]).astype(jnp.bfloat16),
        jnp.zeros((), jnp.bfloat16),
    )
    buffer_shape = (owners, local_experts, capacity, feature_count)
    send_in = send_in.reshape(buffer_shape)
    send_grad = send_grad.reshape(buffer_shape)
    got_in = lax.all_to_all(send_in, "expert", split_axis=0, concat_axis=0, tiled=True)
    gate_pre, up_pre, hidden_act, result = forward_rows(got_in, w_gate, w_up, w_down)
    back_out = lax.all_to_all(result, "expert", split_axis=0, concat_axis=0, tiled=True)
    got_grad = lax.all_to_all(send_grad, "expert", split_axis=0, concat_axis=0, tiled=True)
    input_delta, gate_term, up_term, down_term = backward_rows(
        got_in, gate_pre, up_pre, hidden_act, got_grad, w_gate, w_up, w_down, grad_scale
    )
    back_delta = lax.all_to_all(input_delta, "expert", split_axis=0, concat_axis=0, tiled=True)
    gate_grad, up_grad, down_grad = (
        lax.psum_scatter(
            gate_term.astype(jnp.bfloat16), "dp", scatter_dimension=1, tiled=True
        ).astype(jnp.float32),
        lax.psum_scatter(
            up_term.astype(jnp.bfloat16), "dp", scatter_dimension=1, tiled=True
        ).astype(jnp.float32),
        lax.psum_scatter(
            down_term.astype(jnp.bfloat16), "dp", scatter_dimension=1, tiled=True
        ).astype(jnp.float32),
    )
    take_out = back_out.reshape(expert_total * capacity, feature_count)[target].reshape(
        tok_rows, top_count, feature_count
    )
    take_delta = back_delta.reshape(expert_total * capacity, feature_count)[target].reshape(
        tok_rows, top_count, feature_count
    )
    moe_out = jnp.sum(route_weights[..., None] * take_out.astype(jnp.float32), axis=1).astype(
        jnp.bfloat16
    )
    route_grad = jnp.einsum("tkd,td->tk", take_out, out_grad, preferred_element_type=jnp.float32)
    norm_delta = jnp.sum(take_delta.astype(jnp.float32), axis=1)
    scaled_delta = norm_delta * norm_gain
    branch = inv_rms * (
        scaled_delta - normed * jnp.mean(scaled_delta * normed, axis=-1, keepdims=True)
    )
    branch_grad = branch.astype(jnp.bfloat16)
    full_grad = (out_grad32 + branch).astype(jnp.bfloat16)
    proj_term = lax.dot_general(
        context, full_grad, (((0,), (0,)), ((), ())), preferred_element_type=jnp.float32
    ) / math.sqrt(token_total)
    gain_term = jnp.sum(norm_delta * normed, axis=0) * grad_scale
    proj_grad, gain_grad = (
        lax.psum_scatter(proj_term, ("expert", "dp"), scatter_dimension=0, tiled=True),
        lax.psum_scatter(gain_term, ("expert", "dp"), scatter_dimension=0, tiled=True),
    )
    return (moe_out, branch_grad, route_grad, gain_grad, proj_grad, gate_grad, up_grad, down_grad)


def spread_kernel(a_in, b_in, a_all, b_all, own_sem, send_sem, recv_sem):
    parts, owners = a_all.shape[:2]
    at, line = lax.axis_index("expert"), lax.axis_index("dp")
    sibling = at + 1 - 2 * lax.rem(at, 2)
    across = lax.rem(at + 2, owners)
    sibling_across = lax.rem(sibling + 2, owners)
    below, above = line > 0, line < parts - 1
    always = line >= 0
    partner = {
        "across": (across, line, always),
        "above": (at, line + 1, above),
        "below": (at, line - 1, below),
        "sibling": (sibling, line, always),
    }
    names = list(partner)
    barrier = pltpu.get_barrier_semaphore()
    for name in names:
        to, to_line, cond = partner[name]

        @pl.when(cond)
        def _():
            pl.semaphore_signal(
                barrier,
                inc=1,
                device_id={"expert": to, "dp": to_line},
                device_id_type=pl.DeviceIdType.MESH,
            )

    neighbours = lax.div(line + parts - 1, parts) + lax.div(2 * parts - 2 - line, parts)
    pl.semaphore_wait(barrier, 2 + neighbours)

    buffers = (a_all, b_all)
    started = []

    def copy(which, of, of_line, name, source):
        to, to_line, _ = partner[name]
        place = buffers[which].at[of_line, of]
        return pltpu.make_async_remote_copy(
            src_ref=place if source is None else source,
            dst_ref=place,
            send_sem=send_sem.at[which, of_line, of, names.index(name)],
            recv_sem=recv_sem.at[which, of_line, of],
            device_id={"expert": to, "dp": to_line},
            device_id_type=pl.DeviceIdType.MESH,
        )

    def push(which, of, of_line, there, name, source=None):
        cond = jnp.logical_and(there, partner[name][2])

        @pl.when(cond)
        def _():
            copy(which, of, of_line, name, source).start()

        started.append((which, of, of_line, cond, name, source))

    def arrived(which, of, of_line, there):
        @pl.when(there)
        def _():
            copy(which, of, of_line, "sibling", None).wait_recv()

    def relay(which, of, of_line, there, targets):
        arrived(which, of, of_line, there)
        for name in targets:
            push(which, of, of_line, there, name)

    mine = [
        pltpu.make_async_copy(source, buffer.at[line, at], own_sem.at[i])
        for i, (source, buffer) in enumerate(((a_in, a_all), (b_in, b_all)))
    ]
    for name in ("above", "below", "across", "sibling"):
        push(0, at, line, always, name, a_in)
        push(1, at, line, always, name, b_in)
    for copy_in in mine:
        copy_in.start()
    for step in range(1, parts + 1):
        low, high = line - step, line + step
        has_low, has_high = low >= 0, high < parts
        low1, high1 = line - (step - 1), line + (step - 1)
        has_low1, has_high1 = low1 >= 0, high1 < parts
        if step < parts:
            relay(0, at, low, has_low, ("above", "across", "sibling"))
            relay(0, at, high, has_high, ("below", "across", "sibling"))
        if step == 1:
            relay(1, across, line, always, ("above", "below", "sibling"))
        else:
            relay(1, across, low1, has_low1, ("above", "sibling"))
            relay(1, across, high1, has_high1, ("below", "sibling"))
        if step < parts:
            relay(1, at, low, has_low, ("above", "sibling"))
            relay(1, at, high, has_high, ("below", "sibling"))
        if step == 1:
            relay(0, across, line, always, ("sibling",))
        else:
            relay(0, across, low1, has_low1, ("sibling",))
            relay(0, across, high1, has_high1, ("sibling",))
    for of_line in range(parts):
        for of in (sibling, sibling_across):
            for which in range(2):
                arrived(which, of, of_line, always)
    for which, of, of_line, cond, name, source in started:

        @pl.when(cond)
        def _():
            copy(which, of, of_line, name, source).wait_send()

    for copy_in in mine:
        copy_in.wait()


def spread(a_block, b_block, parts, owners):
    any_space = pl.BlockSpec(memory_space=pl.ANY)
    return pl.pallas_call(
        spread_kernel,
        out_shape=[
            jax.ShapeDtypeStruct((parts, owners, *block.shape), block.dtype)
            for block in (a_block, b_block)
        ],
        in_specs=[any_space, any_space],
        out_specs=[any_space, any_space],
        scratch_shapes=[
            pltpu.SemaphoreType.DMA((2,)),
            pltpu.SemaphoreType.DMA((2, parts, owners, 4)),
            pltpu.SemaphoreType.DMA((2, parts, owners)),
        ],
        compiler_params=pltpu.CompilerParams(collective_id=0, has_side_effects=True),
    )(a_block, b_block)


def three_terms(value):
    high = lax.reduce_precision(value, 8, 7)
    middle = lax.reduce_precision(value - high, 8, 7)
    low = value - high - middle
    return [term.astype(jnp.bfloat16) for term in (high, middle, low)]


def expert_kernel(
    grad_scale, in_ref, raw_ref, weight_ref, gate_ref, up_ref, down_ref,
    gate_grad, up_grad, down_grad, result, input_delta, act, gate_delta, up_delta,
):
    parts, _, super_rows, features = in_ref.shape
    part = lax.axis_index("dp")
    rows = parts * super_rows
    cols, units = gate_grad.shape[1], down_grad.shape[1]

    def dot(a, b, a_dim, b_dim):
        return lax.dot_general(
            a, b, (((a_dim,), (b_dim,)), ((), ())), preferred_element_type=jnp.float32
        )

    rows_in = in_ref[...].reshape(rows, features)
    raw = raw_ref[...].reshape(rows, features).astype(jnp.float32)
    rows_grad = (weight_ref[0] * raw).astype(jnp.bfloat16)
    gate_pre = dot(rows_in, gate_ref[0], 1, 0)
    up_pre = dot(rows_in, up_ref[0], 1, 0)
    inner = dot(rows_grad, down_ref[0], 1, 1)
    logistic = jax.nn.sigmoid(gate_pre)
    silu = gate_pre * logistic
    act[...] = (silu * up_pre).astype(jnp.bfloat16)
    slope = logistic * (1.0 + gate_pre * (1.0 - logistic))
    gate_delta[...] = (inner * up_pre * slope).astype(jnp.bfloat16)
    up_delta[...] = (inner * silu).astype(jnp.bfloat16)
    cut_in = in_ref[:, 0, :, pl.ds(pl.multiple_of(part * cols, cols), cols)].reshape(rows, cols)
    cut_act = act[:, pl.ds(pl.multiple_of(part * units, units), units)]
    gate_grad[0] = dot(cut_in, gate_delta[...], 0, 0) * grad_scale
    up_grad[0] = dot(cut_in, up_delta[...], 0, 0) * grad_scale
    down_grad[0] = dot(cut_act, rows_grad, 0, 0) * grad_scale
    own = pl.ds(pl.multiple_of(part * super_rows, super_rows), super_rows)
    result[0] = dot(act[own, :], down_ref[0], 1, 0).astype(jnp.bfloat16)
    input_delta[0] = (
        dot(gate_delta[own, :], gate_ref[0], 1, 1) + dot(up_delta[own, :], up_ref[0], 1, 1)
    ).astype(jnp.bfloat16)


def run_experts(rows_in, raw_grad, slot_weight, w_gate, w_up, w_down, grad_scale):
    parts, local_experts, super_rows, features = rows_in.shape
    hidden_units = w_gate.shape[2]
    rows = parts * super_rows
    block = lambda *shape: pl.BlockSpec((1, *shape), lambda j: (j, 0, 0))
    slots = pl.BlockSpec((parts, 1, super_rows, features), lambda j: (0, j, 0, 0))
    whole = lambda kind, *shape: jax.ShapeDtypeStruct((local_experts, *shape), kind)
    cols, units = features // parts, hidden_units // parts
    return pl.pallas_call(
        functools.partial(expert_kernel, grad_scale),
        grid=(local_experts,),
        in_specs=[
            slots,
            slots,
            block(rows, 1),
            block(features, hidden_units),
            block(features, hidden_units),
            block(hidden_units, features),
        ],
        out_specs=[
            block(cols, hidden_units),
            block(cols, hidden_units),
            block(units, features),
            block(super_rows, features),
            block(super_rows, features),
        ],
        out_shape=[
            whole(jnp.float32, cols, hidden_units),
            whole(jnp.float32, cols, hidden_units),
            whole(jnp.float32, units, features),
            whole(jnp.bfloat16, super_rows, features),
            whole(jnp.bfloat16, super_rows, features),
        ],
        scratch_shapes=[pltpu.VMEM((rows, hidden_units), jnp.bfloat16)] * 3,
        compiler_params=pltpu.CompilerParams(vmem_limit_bytes=48 * 2**20),
    )(rows_in, raw_grad, slot_weight, w_gate, w_up, w_down)


def token_rows(ids, local_experts, capacity, first_expert):
    blocks, owners, tok_rows, _ = ids.shape
    named = first_expert + jnp.arange(local_experts, dtype=jnp.int32)
    hit = jnp.any(ids[..., None] == named, axis=3)
    order = jnp.arange(tok_rows)
    before = (order[:, None] > order[None, :]).astype(jnp.bfloat16)
    position = jnp.einsum(
        "ut,sbtj->sbuj", before, hit.astype(jnp.bfloat16), preferred_element_type=jnp.float32
    ).astype(jnp.int32)
    base = jnp.arange(owners, dtype=jnp.int32)[None, :, None, None] * capacity
    row = jnp.where(hit, base + position, -1)
    return row.reshape(blocks, owners * tok_rows, local_experts)


def gathered_body(hidden_in, context, norm_gain, route_ids, route_weights, w_gate, w_up, w_down, out_grad):
    tok_rows, feature_count = hidden_in.shape
    top_count = route_ids.shape[1]
    local_experts = w_gate.shape[0]
    owners, parts = lax.axis_size("expert"), lax.axis_size("dp")
    expert_at, part_at = lax.axis_index("expert"), lax.axis_index("dp")
    capacity = tok_rows * top_count * 9 // (8 * local_experts * owners)
    token_total = tok_rows * owners * parts
    grad_scale = 8.0 / math.sqrt(token_total)
    super_toks, super_rows = owners * tok_rows, owners * capacity
    hidden = hidden_in.astype(jnp.float32)
    inv_rms = lax.rsqrt(jnp.mean(hidden * hidden, axis=-1, keepdims=True) + EPSILON)
    normed = hidden * inv_rms
    scaled_in = (normed * norm_gain).astype(jnp.bfloat16)

    routes = jnp.concatenate([route_ids.astype(jnp.bfloat16), *three_terms(route_weights)], axis=1)
    routes = jnp.pad(routes, ((0, 0), (0, -routes.shape[1] % 128)))
    tok_in, tok_grad = spread(
        jnp.concatenate([scaled_in, routes], axis=1), out_grad, parts, owners
    )
    tok_in = tok_in.reshape(parts, super_toks, -1)
    tok_grad = tok_grad.reshape(parts, super_toks, feature_count)
    routes = tok_in[..., feature_count:].astype(jnp.float32)
    tok_in = tok_in[..., :feature_count]
    terms = [routes[..., i * top_count : (i + 1) * top_count] for i in range(4)]
    ids = terms[0].astype(jnp.int32)
    weights = terms[1] + terms[2] + terms[3]
    first_expert = expert_at * local_experts
    row = token_rows(
        ids.reshape(parts, owners, tok_rows, top_count), local_experts, capacity, first_expert
    )
    named = first_expert + jnp.arange(local_experts, dtype=jnp.int32)
    match = ids[..., None] == named
    tok_weight = jnp.sum(jnp.where(match, weights[..., None], 0.0), axis=2)
    slots = jnp.arange(super_rows, dtype=jnp.int32)
    pick_mask = row.transpose(0, 2, 1)[:, :, None, :] == slots[:, None]
    pick = pick_mask.astype(jnp.bfloat16)
    slot_weight = jnp.sum(
        jnp.where(pick_mask, tok_weight.transpose(0, 2, 1)[:, :, None, :], 0.0), axis=-1
    )
    slot_weight = slot_weight.transpose(1, 0, 2).reshape(local_experts, parts * super_rows, 1)
    dot = lambda spec, a, b: jnp.einsum(spec, a, b, preferred_element_type=jnp.float32)
    flat_pick = pick.reshape(parts, local_experts * super_rows, super_toks)
    slot_shape = (parts, local_experts, super_rows, feature_count)
    rows_in = dot("srt,std->srd", flat_pick, tok_in).astype(jnp.bfloat16).reshape(slot_shape)
    raw_grad = dot("srt,std->srd", flat_pick, tok_grad).astype(jnp.bfloat16).reshape(slot_shape)
    gate_grad, up_grad, down_grad, result, input_delta = run_experts(
        rows_in, raw_grad, slot_weight, w_gate, w_up, w_down, grad_scale
    )
    own_pick = lax.dynamic_index_in_dim(pick, part_at, axis=0, keepdims=False)
    own_weight = lax.dynamic_index_in_dim(tok_weight, part_at, axis=0, keepdims=False)
    own_match = lax.dynamic_index_in_dim(match, part_at, axis=0, keepdims=False)
    own_raw = lax.dynamic_index_in_dim(raw_grad, part_at, axis=0, keepdims=False)
    own_raw = own_raw.astype(jnp.float32)
    weighted = own_pick * own_weight.T.astype(jnp.bfloat16)[:, None, :]
    moe_term = dot("jct,jcd->td", weighted, result).astype(jnp.bfloat16)
    delta_term = dot("jct,jcd->td", own_pick, input_delta).astype(jnp.bfloat16)
    slot_route = jnp.sum(own_raw * result.astype(jnp.float32), axis=-1)
    tok_route = jnp.sum(jnp.where(own_pick > 0, slot_route[..., None], 0.0), axis=1)
    route_term = jnp.sum(jnp.where(own_match, tok_route.T[:, None, :], 0.0), axis=-1)

    def scatter(term):
        cut = term.reshape(owners, tok_rows, -1)
        got = lax.all_to_all(cut, "expert", split_axis=0, concat_axis=0, tiled=True)
        return jnp.sum(got.astype(jnp.float32), axis=0)

    norm_delta = scatter(delta_term)
    moe_out = scatter(moe_term).astype(jnp.bfloat16)
    route_grad = scatter(route_term)

    scaled_delta = norm_delta * norm_gain
    branch = inv_rms * (
        scaled_delta - normed * jnp.mean(scaled_delta * normed, axis=-1, keepdims=True)
    )
    branch_grad = branch.astype(jnp.bfloat16)
    full_grad = (out_grad.astype(jnp.float32) + branch).astype(jnp.bfloat16)
    proj_term = lax.dot_general(
        context, full_grad, (((0,), (0,)), ((), ())), preferred_element_type=jnp.float32
    ) / math.sqrt(token_total)
    gain_term = jnp.sum(norm_delta * normed, axis=0) * grad_scale
    gain_cols = jnp.stack(three_terms(gain_term), axis=1)
    gain_cols = jnp.pad(gain_cols, ((0, 0), (0, 125)))
    both = jnp.concatenate([proj_term.astype(jnp.bfloat16), gain_cols], axis=1)
    both = lax.psum_scatter(both, ("expert", "dp"), scatter_dimension=0, tiled=True)
    both = both.astype(jnp.float32)
    proj_grad = both[:, :feature_count]
    gain_grad = jnp.sum(both[:, feature_count:], axis=1)
    return (moe_out, branch_grad, route_grad, gain_grad, proj_grad, gate_grad, up_grad, down_grad)


def body(*args):
    few = lax.axis_size("dp") <= 4 and lax.axis_size("expert") == 4
    return (gathered_body if few else scattered_body)(*args)


def solution(mesh):
    return jax.shard_map(
        body,
        mesh=mesh,
        in_specs=(
            P(("groups", "expert", "dp"), None),
            P(("groups", "expert", "dp"), None),
            P(),
            P(("groups", "expert", "dp"), None),
            P(("groups", "expert", "dp"), None),
            P("expert", None, None),
            P("expert", None, None),
            P("expert", None, None),
            P(("groups", "expert", "dp"), None),
        ),
        out_specs=(
            P(("groups", "expert", "dp"), None),
            P(("groups", "expert", "dp"), None),
            P(("groups", "expert", "dp"), None),
            P(("groups", "expert", "dp")),
            P(("groups", "expert", "dp"), None),
            P(("groups", "expert"), "dp", None),
            P(("groups", "expert"), "dp", None),
            P(("groups", "expert"), "dp", None),
        ),
        check_vma=False,
    )
```
